32 devices in a mesh: groups: 2 (over y), pb: 16 (over z, x, core).
Axes of the slice: x: 2, y: 2, z: 4, core: 2. Of those that a mesh axis runs over, the one named last changes fastest.
Arguments:
- fields: float32 [32, 16, 512], P(('groups', 'pb')), parts along dimension 0, may hold values from -6 to 6
- field_shift: float32 [16, 512], replicated, may hold values from -1 to 1
- cholesky: bfloat16 [512, 1024, 1024], P(None, 'pb'), may hold values from -0.015625 to 0.015625
- onebody: float32 [16, 64], replicated, may hold values from -0.5 to 0.5
- walkers: bfloat16 [32, 1024, 256], P(('groups', 'pb')), parts along dimension 0, may hold values from -6 to 6
Outputs:
- propagated: bfloat16 [32, 1024, 256], P(('groups', 'pb')), parts along dimension 0
The draws below stay inside these ranges and needn't reach their ends.
There are 2 independent parts, one for each index of `groups`. The reference program is written for one: setup_inputs(seed, part) draws one part's arguments, and reference() takes and returns one part's arrays. A program takes and returns all parts, laid end to end along the dimension named above; an argument that names none is the same for every part. Nothing has to cross between parts.
All inputs are finite; a program needn't handle non-finite values.
Results may differ from the reference program's by a relative error of at most 0.0089.
Values may be sent and summed in bfloat16 or wider, within the bound.
No kernel may reach another device: no remote copies, remote signals or barrier semaphores. Data moves between devices by JAX's collectives and lax.ppermute only.
A program may use at most 192 MiB of HBM per device.

```python
import jax
import jax.numpy as jnp
from jax import lax

NK = 16
NORB = 64
NCHOL = 512
COLS = 256
TERMS = 6
WALKERS = 16


def level_of(key, shape, shards, smallest, largest):
    factor_of = 1.0
    for position, shards_of in shards:
        steps = jax.random.uniform(jax.random.fold_in(jax.random.fold_in(key, 6), position), (shards_of,), jnp.float32, smallest / len(shards), largest / len(shards))
        factor_of = factor_of * jnp.repeat(jnp.exp(steps), shape[position] // shards_of).reshape((-1,) + (1,) * (len(shape) - 1 - position))
    return factor_of


def gaussian(stream_key, extent, width, bound, shards=(), dtype=jnp.bfloat16):
    level = level_of(stream_key, extent, shards, -0.22, 0.18) if shards else 1.0
    entries = jax.random.normal(stream_key, extent, jnp.float32) * width * level
    return jnp.minimum(jnp.maximum(entries, -bound), bound).astype(dtype)


def setup_inputs(seed: int = 0, part: int = 0) -> dict:
    keys = jax.random.split(jax.random.key(seed), 6)
    part_splits = jax.random.split(jax.random.fold_in(keys[5], part), 6)
    return {
        "fields": gaussian(part_splits[0], (WALKERS, NK, NCHOL), 1.0, 6.0, ((0, 16),), jnp.float32),
        "field_shift": jnp.clip(jax.random.uniform(keys[1], (NK, NCHOL), jnp.float32, -1.0, 1.0), -1.0, 1.0),
        "cholesky": gaussian(keys[2], (NCHOL, NK * NORB, NK * NORB), (NCHOL * NK * NORB // 4) ** -0.5, 0.015625, ((1, 16),)),
        "onebody": jnp.clip(jax.random.uniform(keys[3], (NK, NORB), jnp.float32, -0.5, 0.5), -0.5, 0.5),
        "walkers": gaussian(part_splits[4], (WALKERS, NK * NORB, COLS), 1.0, 6.0, ((0, 16),)),
    }


def taylor(potential, determinant, onebody):
    term = determinant
    total = determinant.astype(jnp.float32)
    for order in range(1, TERMS):
        rolled = jnp.stack([jnp.roll(term, transfer, axis=0) for transfer in range(NK)], axis=1)
        rolled = rolled.reshape(NK, NK * NORB, COLS)
        product = jnp.einsum("kaj,kjc->kac", potential.astype(jnp.float32), rolled.astype(jnp.float32), precision=lax.Precision.HIGHEST)
        product = product + onebody[:, :, None] * term.astype(jnp.float32)
        term = (product * (-1.0 / order)).astype(jnp.bfloat16)
        total = total + term.astype(jnp.float32)
    return total.astype(jnp.bfloat16)


def reference(fields, field_shift, cholesky, onebody, walkers):
    count = fields.shape[0]
    shifted = (fields + field_shift[None]).astype(jnp.bfloat16)
    blocks = []
    for transfer in range(NK):
        slab = cholesky[:, transfer * NORB:(transfer + 1) * NORB, :].reshape(NCHOL, NORB * NK * NORB)
        blocks.append(jnp.dot(shifted[:, transfer, :], slab, preferred_element_type=jnp.float32).astype(jnp.bfloat16))
    potential_all = jnp.stack(blocks, axis=1).reshape(count, NK, NORB, NK, NORB)

    def propagate(pair):
        blocks_one, determinant = pair
        potential = blocks_one.transpose(2, 1, 0, 3).reshape(NK, NORB, NK * NORB)
        result = taylor(potential, determinant.reshape(NK, NORB, COLS), onebody)
        return result.reshape(NK * NORB, COLS)

    return lax.map(propagate, (potential_all, walkers))
```

```python
import functools

import jax
import jax.numpy as jnp
from jax import lax
from jax.experimental import pallas as pl
from jax.experimental.pallas import tpu as pltpu
from jax.sharding import PartitionSpec as P

TERMS = 6
LANES = 128
VMEM_LIMIT = 56 * 1024 * 1024


def shift_kernel(fields_ref, shift_ref, out_ref):
    shifted = (fields_ref[...] + shift_ref[...]).astype(jnp.bfloat16).astype(jnp.float32)
    for v in range(out_ref.shape[1]):
        out_ref[:, v, :] = shifted[:, v * LANES:(v + 1) * LANES]


def shift_fields(fields, field_shift):
    kpoints, vectors = field_shift.shape
    return pl.pallas_call(
        shift_kernel,
        out_shape=jax.ShapeDtypeStruct((kpoints, vectors // LANES, LANES), jnp.float32),
    )(fields, field_shift)


def potential_kernel(shifted_ref, slab_ref, out_ref, total):
    step = pl.program_id(1)
    walkers = shifted_ref.shape[0]
    vectors, rows, columns = slab_ref.shape
    depth = vectors * rows
    spread = (
        lax.broadcasted_iota(jnp.int32, (vectors, depth), 1) // rows
        == lax.broadcasted_iota(jnp.int32, (vectors, depth), 0)
    )
    spread = jnp.where(spread, 1.0, 0.0).astype(jnp.bfloat16)
    shifted = shifted_ref[:, step, :].astype(jnp.bfloat16)
    wide = jnp.dot(shifted, spread, preferred_element_type=jnp.float32)
    same = (
        lax.broadcasted_iota(jnp.int32, (rows, depth), 1) % rows
        == lax.broadcasted_iota(jnp.int32, (rows, depth), 0)
    )
    left = jnp.concatenate(
        [
            jnp.where(same, jnp.broadcast_to(wide[w:w + 1], (rows, depth)), 0.0).astype(jnp.bfloat16)
            for w in range(walkers)
        ],
        axis=0,
    )
    part = jnp.dot(left, slab_ref[...].reshape(depth, columns), preferred_element_type=jnp.float32)

    @pl.when(step == 0)
    def _():
        total[...] = part

    @pl.when(step > 0)
    def _():
        total[...] += part

    @pl.when(step == pl.num_programs(1) - 1)
    def _():
        out_ref[...] = total[...].astype(jnp.bfloat16).reshape(out_ref.shape)


def potential_rows(shifted, slab, first, count, block_rows):
    walkers, steps, lanes = shifted.shape
    vectors, _, columns = slab.shape
    return pl.pallas_call(
        potential_kernel,
        grid=(count // block_rows, steps),
        in_specs=[
            pl.BlockSpec((walkers, steps, lanes), lambda i, g: (0, 0, 0)),
            pl.BlockSpec((lanes, block_rows, columns), lambda i, g: (g, first // block_rows + i, 0)),
        ],
        out_specs=pl.BlockSpec((walkers, block_rows, columns), lambda i, g: (0, i, 0)),
        out_shape=jax.ShapeDtypeStruct((walkers, count, columns), jnp.bfloat16),
        scratch_shapes=[pltpu.VMEM((walkers * block_rows, columns), jnp.float32)],
        compiler_params=pltpu.CompilerParams(vmem_limit_bytes=VMEM_LIMIT),
        cost_estimate=pl.CostEstimate(
            flops=2 * walkers * count * block_rows * vectors * columns,
            bytes_accessed=2 * count * vectors * columns,
            transcendentals=0,
        ),
    )(shifted, slab)


def taylor_kernel(kpoints, *refs):
    block_refs = refs[:-5]
    onebody_ref, walker_ref, out_ref, matrix, term = refs[-5:]
    size = matrix.shape[0]
    orbitals = size // kpoints
    per_tile = LANES // orbitals
    first = 0
    for block in block_refs:
        rows = block.shape[1]
        for k in range(kpoints):
            lanes = slice(k * orbitals, (k + 1) * orbitals)
            for tile in range(size // LANES):
                sources = [(k - tile * per_tile - i) % kpoints for i in range(per_tile)]
                matrix[k * orbitals + first:k * orbitals + first + rows, tile * LANES:(tile + 1) * LANES] = (
                    jnp.concatenate([block[q, :, lanes] for q in sources], axis=1)
                )
        first += rows
    term[...] = walker_ref[...]
    total = walker_ref[...].astype(jnp.float32)
    for order in range(1, TERMS):
        product = jnp.dot(matrix[...], term[...], preferred_element_type=jnp.float32)
        product = product + onebody_ref[...] * term[...].astype(jnp.float32)
        term[...] = (product * (-1.0 / order)).astype(jnp.bfloat16)
        total = total + term[...].astype(jnp.float32)
    out_ref[...] = total.astype(jnp.bfloat16)


def taylor(blocks, onebody, walker):
    kpoints, orbitals = onebody.shape
    size, columns = walker.shape
    return pl.pallas_call(
        functools.partial(taylor_kernel, kpoints),
        out_shape=jax.ShapeDtypeStruct(walker.shape, jnp.bfloat16),
        scratch_shapes=[
            pltpu.VMEM((size, size), jnp.bfloat16),
            pltpu.VMEM((size, columns), jnp.bfloat16),
        ],
        compiler_params=pltpu.CompilerParams(vmem_limit_bytes=VMEM_LIMIT),
        cost_estimate=pl.CostEstimate(
            flops=2 * (TERMS - 1) * size * size * columns,
            bytes_accessed=2 * size * (size + 2 * columns),
            transcendentals=0,
        ),
    )(*blocks, onebody.reshape(size, 1), walker)


def per_device(fields, field_shift, cholesky, onebody, walkers):
    devices = lax.axis_size("pb")
    local_walkers = fields.shape[0]
    kpoints, orbitals = onebody.shape
    vectors, rows_here, columns = cholesky.shape
    per_transfer = orbitals // rows_here
    block_rows = min(16, rows_here)
    chunks = CHUNKS if rows_here % (16 * CHUNKS) == 0 else 1

    outgoing = jnp.stack([shift_fields(fields[w], field_shift) for w in range(local_walkers)], axis=1)
    outgoing = jnp.repeat(outgoing, per_transfer, axis=0)
    arrived = lax.all_to_all(outgoing, "pb", split_axis=0, concat_axis=0, tiled=True)
    arrived = arrived.reshape((devices * local_walkers,) + arrived.shape[2:])

    count = rows_here // chunks
    relayed = []
    for chunk in range(chunks):
        blocks = potential_rows(arrived, cholesky, chunk * count, count, block_rows)
        blocks = blocks.reshape(devices, local_walkers, count, columns)
        relayed.append(lax.all_to_all(blocks, "pb", split_axis=0, concat_axis=0, tiled=True))

    results = []
    for w in range(local_walkers):
        mine = [r[:, w].reshape(kpoints, per_transfer * count, columns) for r in relayed]
        results.append(taylor(mine, onebody, walkers[w]))
    return jnp.stack(results, axis=0)


CHUNKS = 4


def solution(mesh):
    return jax.shard_map(
        per_device,
        mesh=mesh,
        in_specs=(
            P(("groups", "pb"), None, None),
            P(),
            P(None, "pb", None),
            P(),
            P(("groups", "pb"), None, None),
        ),
        out_specs=P(("groups", "pb"), None, None),
        check_vma=False,
    )
```

```python
import functools

import jax
import jax.numpy as jnp
from jax import lax
from jax.experimental import pallas as pl
from jax.experimental.pallas import tpu as pltpu
from jax.sharding import PartitionSpec as P

TERMS = 6
LANES = 128
STRIP = 8
PART = 128
VMEM_LIMIT = 56 * 1024 * 1024
MIDDLE_VMEM_LIMIT = 24 * 1024 * 1024
SMALL_VMEM_LIMIT = 8 * 1024 * 1024


def shift_kernel(fields_ref, shift_ref, out_ref):
    shifted = (fields_ref[...] + shift_ref[...]).astype(jnp.bfloat16).astype(jnp.float32)
    for v in range(out_ref.shape[1]):
        out_ref[:, v, :] = shifted[:, v * LANES:(v + 1) * LANES]


def shift_fields(fields, field_shift):
    kpoints, vectors = field_shift.shape
    return pl.pallas_call(
        shift_kernel,
        out_shape=jax.ShapeDtypeStruct((kpoints, vectors // LANES, LANES), jnp.float32),
    )(fields, field_shift)


def potential_kernel(plan, shifted_ref, slab_ref, *refs):
    offset, count, far, own, devices = plan
    far_refs, all_ref, (slab, left, total, arrived) = refs[:far], refs[far], refs[far + 1:]
    walkers, blocks, _ = shifted_ref.shape
    vectors, _, columns = slab.shape
    parts = vectors // PART
    height = min(16, count)
    me, group = lax.axis_index("pb"), lax.axis_index("groups")
    first = offset if own == slab_ref.shape[1] else pl.multiple_of(group * own + offset, height)

    def fetch(block, part):
        return pltpu.make_async_copy(
            slab_ref.at[pl.ds(part * PART, PART), pl.ds(first + block * height, height)],
            slab.at[pl.ds(part * PART, PART), pl.ds(block * height, height)],
            arrived.at[block, part],
        )

    for block in range(count // height):
        for part in range(parts):
            fetch(block, part).start()

    depth = LANES * STRIP
    spread = (
        lax.broadcasted_iota(jnp.int32, (LANES, depth), 1) // STRIP
        == lax.broadcasted_iota(jnp.int32, (LANES, depth), 0)
    )
    spread = jnp.where(spread, 1.0, 0.0).astype(jnp.bfloat16)
    same = (
        lax.broadcasted_iota(jnp.int32, (STRIP, depth), 1) % STRIP
        == lax.broadcasted_iota(jnp.int32, (STRIP, depth), 0)
    )
    order = far_places(far, devices, group, me) + near_places(walkers - far, devices, me)
    rows_of = [shifted_ref[g * devices + d] for g, d in order]
    for v in range(blocks):
        shifted = jnp.concatenate([row[v:v + 1] for row in rows_of], axis=0).astype(jnp.bfloat16)
        wide = jnp.dot(shifted, spread, preferred_element_type=jnp.float32)
        for pair in range(walkers // 2):
            left[pair * 16:pair * 16 + 16, v * depth:(v + 1) * depth] = jnp.concatenate(
                [
                    jnp.where(same, jnp.broadcast_to(wide[w:w + 1], (STRIP, depth)), 0.0)
                    for w in (2 * pair, 2 * pair + 1)
                ],
                axis=0,
            ).astype(jnp.bfloat16)

    strips = height // STRIP
    for block in range(count // height):
        for part in range(parts):
            fetch(block, part).wait()
            for strip in range(strips):
                top = block * height + strip * STRIP
                product = jnp.dot(
                    left[:, part * PART * STRIP:(part + 1) * PART * STRIP],
                    slab[part * PART:(part + 1) * PART, top:top + STRIP].reshape(PART * STRIP, columns),
                    preferred_element_type=jnp.float32,
                )
                if part == 0:
                    total[strip] = product
                else:
                    total[strip] += product
        for i in range(walkers):
            value = jnp.concatenate(
                [total[strip, i * STRIP:(i + 1) * STRIP] for strip in range(strips)], axis=0
            ).astype(jnp.bfloat16)
            if i < far:
                far_refs[i][block * height:(block + 1) * height] = value
            else:
                all_ref[i - far, block * height:(block + 1) * height] = value


def far_places(far, devices, group, me):
    half = devices // 2
    return [(group ^ (i // half), me ^ (half + i % half)) for i in range(far)]


def near_places(count, devices, me):
    half = devices // 2
    if count % devices:
        return [(j // half, me // half * half + j % half) for j in range(count)]
    if count >= 2 * devices or count == devices:
        return [(j // devices, j % devices) for j in range(count)]


def potential_rows(shifted, slab, plan):
    offset, count, far, own, devices = plan
    walkers, blocks, _ = shifted.shape
    vectors, _, columns = slab.shape
    height = min(16, count)
    return pl.pallas_call(
        functools.partial(potential_kernel, plan),
        in_specs=[pl.BlockSpec(memory_space=pltpu.VMEM), pl.BlockSpec(memory_space=pl.ANY)],
        out_shape=[jax.ShapeDtypeStruct((count, columns), jnp.bfloat16) for _ in range(far)]
        + [jax.ShapeDtypeStruct((walkers - far, count, columns), jnp.bfloat16)],
        scratch_shapes=[
            pltpu.VMEM((vectors, count, columns), slab.dtype),
            pltpu.VMEM((walkers * STRIP, vectors * STRIP), jnp.bfloat16),
            pltpu.VMEM((height // STRIP, walkers * STRIP, columns), jnp.float32),
            pltpu.SemaphoreType.DMA((count // height, vectors // PART)),
        ],
        compiler_params=pltpu.CompilerParams(vmem_limit_bytes=VMEM_LIMIT),
        cost_estimate=pl.CostEstimate(
            flops=2 * walkers * STRIP * count * vectors * columns,
            bytes_accessed=2 * count * vectors * columns,
            transcendentals=0,
        ),
    )(shifted, slab)


def stage(inputs, potential, arrived):
    kpoints, shares, _, _ = potential.shape
    far = len(inputs) - 1
    me, group = lax.axis_index("pb"), lax.axis_index("groups")
    copies = [(inputs[i], potential.at[d, g]) for i, (g, d) in enumerate(far_places(far, kpoints, group, me))]
    each = inputs[far].shape[0] // shares
    base = me // each * each if far else 0
    copies += [
        (inputs[far].at[pl.ds(s * each, each)], potential.at[pl.ds(base, each), s]) for s in range(shares)
    ]
    copies = [pltpu.make_async_copy(a, b, arrived.at[n]) for n, (a, b) in enumerate(copies)]
    for copy in copies:
        copy.start()
    for copy in copies:
        copy.wait()


def arrange(potential, matrix):
    kpoints, shares, rows, size = potential.shape
    orbitals = size // kpoints
    per_tile = LANES // orbitals
    for k in range(kpoints):
        lanes = slice(k * orbitals, (k + 1) * orbitals)
        for tile in range(kpoints // per_tile):
            sources = [(k - tile * per_tile - i) % kpoints for i in range(per_tile)]
            for s in range(shares):
                top = (k * shares + s) * rows
                matrix[top:top + rows, tile * LANES:(tile + 1) * LANES] = jnp.concatenate(
                    [potential[q, s, :, lanes] for q in sources], axis=1
                )


def first_kernel(count, *refs):
    inputs, (walker_ref, matrix, product, potential, arrived) = refs[:count], refs[count:]
    stage(inputs, potential, arrived)
    arrange(potential, matrix)
    product[...] = jnp.dot(matrix[...], walker_ref[...], preferred_element_type=jnp.float32)


def first_rows(inputs, shares, kpoints, walker):
    size, columns = walker.shape
    rows = inputs[-1].shape[1]
    return pl.pallas_call(
        functools.partial(first_kernel, len(inputs)),
        in_specs=[pl.BlockSpec(memory_space=pl.ANY)] * len(inputs) + [pl.BlockSpec(memory_space=pltpu.VMEM)],
        out_shape=[
            jax.ShapeDtypeStruct((kpoints * shares * rows, size), jnp.bfloat16),
            jax.ShapeDtypeStruct((kpoints * shares * rows, columns), jnp.float32),
        ],
        scratch_shapes=[
            pltpu.VMEM((kpoints, shares, rows, size), jnp.bfloat16),
            pltpu.SemaphoreType.DMA((len(inputs) - 1 + shares,)),
        ],
        compiler_params=pltpu.CompilerParams(vmem_limit_bytes=SMALL_VMEM_LIMIT),
        cost_estimate=pl.CostEstimate(
            flops=2 * kpoints * shares * rows * size * columns,
            bytes_accessed=4 * kpoints * shares * rows * size,
            transcendentals=0,
        ),
    )(*inputs, walker)


def taylor_kernel(chunks, count, *refs):
    done = len(chunks) - 1
    inputs, refs = refs[:count], refs[count:]
    sources, refs = refs[:2 * done], refs[2 * done:]
    held, refs = refs[len(refs) - 2 * done:], refs[:len(refs) - 2 * done]
    onebody_ref, walker_ref, out_ref, potential, matrix, term, total, arrived, done_arrived = refs
    kpoints, shares, _, _ = potential.shape
    own = term.shape[1] // shares
    columns = walker_ref.shape[1]
    copies = [pltpu.make_async_copy(a, b, done_arrived.at[n]) for n, (a, b) in enumerate(zip(sources, held))]
    for copy in copies:
        copy.start()
    stage(inputs, potential, arrived)
    arrange(potential, matrix)
    term[...] = walker_ref[...].reshape(term.shape)
    total[...] = term[...].astype(jnp.float32)
    for copy in copies:
        copy.wait()
    matrices = list(held[::2]) + [matrix]
    for order in range(1, TERMS):
        now = term[...].reshape(walker_ref.shape)
        new = [
            held[2 * i + 1][...] if order == 1 and i < done
            else jnp.dot(m[...], now, preferred_element_type=jnp.float32)
            for i, m in enumerate(matrices)
        ]
        for (first, rows), product in zip(chunks, new):
            product = product.reshape(kpoints, shares, rows, columns)
            for s in range(shares):
                here = slice(s * own + first, s * own + first + rows)
                value = product[:, s] + onebody_ref[:, here] * term[:, here].astype(jnp.float32)
                value = (value * (-1.0 / order)).astype(jnp.bfloat16)
                term[:, here] = value
                total[:, here] += value.astype(jnp.float32)
    out_ref[...] = total[...].astype(jnp.bfloat16).reshape(out_ref.shape)


def taylor(inputs, shares, chunks, done, onebody, walker):
    kpoints, orbitals = onebody.shape
    size, columns = walker.shape
    rows = inputs[-1].shape[1]
    whole, anywhere = pl.BlockSpec(memory_space=pltpu.VMEM), pl.BlockSpec(memory_space=pl.ANY)
    parts = [part for pair in done for part in pair]
    return pl.pallas_call(
        functools.partial(taylor_kernel, chunks, len(inputs)),
        in_specs=[anywhere] * (len(inputs) + len(parts)) + [whole] * 2,
        out_shape=jax.ShapeDtypeStruct(walker.shape, jnp.bfloat16),
        scratch_shapes=[
            pltpu.VMEM((kpoints, shares, rows, size), jnp.bfloat16),
            pltpu.VMEM((kpoints * shares * rows, size), jnp.bfloat16),
            pltpu.VMEM((kpoints, orbitals, columns), jnp.bfloat16),
            pltpu.VMEM((kpoints, orbitals, columns), jnp.float32),
            pltpu.SemaphoreType.DMA((len(inputs) - 1 + shares,)),
            pltpu.SemaphoreType.DMA((max(len(parts), 1),)),
        ]
        + [pltpu.VMEM(part.shape, part.dtype) for part in parts],
        compiler_params=pltpu.CompilerParams(vmem_limit_bytes=MIDDLE_VMEM_LIMIT),
        cost_estimate=pl.CostEstimate(
            flops=2 * (TERMS - 1) * size * size * columns,
            bytes_accessed=2 * size * (size + 2 * columns),
            transcendentals=0,
        ),
    )(*inputs, *parts, onebody.reshape(kpoints, orbitals, 1), walker)


def exchange(blocks, axes):
    return lax.all_to_all(blocks, axes, split_axis=0, concat_axis=0, tiled=True)


def per_device(fields, field_shift, cholesky, onebody, walkers):
    devices, groups = lax.axis_size("pb"), lax.axis_size("groups")
    local_walkers = fields.shape[0]
    kpoints, orbitals = onebody.shape
    vectors, rows_here, columns = cholesky.shape
    per_transfer = orbitals // rows_here

    shares = groups if local_walkers == 1 and per_transfer == 1 and rows_here % (16 * groups) == 0 else 1
    axes = ("groups", "pb") if shares > 1 else "pb"
    outgoing = jnp.stack([shift_fields(fields[w], field_shift) for w in range(local_walkers)], axis=1)
    outgoing = jnp.tile(jnp.repeat(outgoing, per_transfer, axis=0), (shares, 1, 1, 1))
    arrived = exchange(outgoing, axes)
    arrived = arrived.reshape((shares * devices * local_walkers,) + arrived.shape[2:])

    own = rows_here // shares
    if shares > 1:
        (blocks,) = potential_rows(arrived, cholesky, (0, own, 0, own, devices))
        return taylor([exchange(blocks, axes)], shares, [(0, own)], [], onebody, walkers[0])[None]

    (blocks,) = potential_rows(arrived, cholesky, (0, own, 0, own, devices))
    relayed = exchange(blocks.reshape(devices, local_walkers, rows_here, columns), axes)
    results = [
        taylor(
            [relayed[:, w].reshape(kpoints, orbitals, columns)], 1, [(0, orbitals)], [], onebody, walkers[w]
        )
        for w in range(local_walkers)
    ]
    return jnp.stack(results, axis=0)


def solution(mesh):
    return jax.shard_map(
        per_device,
        mesh=mesh,
        in_specs=(
            P(("groups", "pb"), None, None),
            P(),
            P(None, "pb", None),
            P(),
            P(("groups", "pb"), None, None),
        ),
        out_specs=P(("groups", "pb"), None, None),
        check_vma=False,
    )
```

```python
import jax
import jax.numpy as jnp
from jax import lax
from jax.experimental import pallas as pl
from jax.experimental.pallas import tpu as pltpu
from jax.sharding import PartitionSpec as P

TERMS = 6
LANES = 128
STRIP = 8
PART = 128
BAND = 4
MIB = 1024 * 1024


def shift_kernel(fields_ref, shift_ref, out_ref, fields, shift, arrived):
    copies = [
        pltpu.make_async_copy(fields_ref, fields, arrived.at[0]),
        pltpu.make_async_copy(shift_ref, shift, arrived.at[1]),
    ]
    for copy in copies:
        copy.start()
    for copy in copies:
        copy.wait()
    shifted = (fields[...] + shift[...]).astype(jnp.bfloat16).astype(jnp.float32)
    for copy in range(out_ref.shape[0]):
        for v in range(out_ref.shape[2]):
            out_ref[copy, :, v, :] = shifted[:, v * LANES:(v + 1) * LANES]


def shift_fields(fields, field_shift, copies):
    kpoints, vectors = field_shift.shape
    return pl.pallas_call(
        shift_kernel,
        in_specs=[pl.BlockSpec(memory_space=pl.ANY)] * 2,
        out_shape=jax.ShapeDtypeStruct((copies, kpoints, vectors // LANES, LANES), jnp.float32),
        scratch_shapes=[
            pltpu.VMEM(fields.shape, jnp.float32),
            pltpu.VMEM(field_shift.shape, jnp.float32),
            pltpu.SemaphoreType.DMA((2,)),
        ],
        compiler_params=pltpu.CompilerParams(vmem_limit_bytes=8 * MIB),
    )(fields, field_shift)


def potential_kernel(shifted_ref, slab_ref, out_ref, slab, left, total, arrived):
    walkers, blocks, _ = shifted_ref.shape
    vectors, rows, columns = slab.shape
    row_blocks, parts = arrived.shape
    height = rows // row_blocks
    strips = height // STRIP
    whole = rows == slab_ref.shape[1]
    first = 0 if whole else pl.multiple_of(lax.axis_index("groups") * rows, rows)

    def fetch(block, part):
        return pltpu.make_async_copy(
            slab_ref.at[pl.ds(part * PART, PART), pl.ds(first + block * height, height)],
            slab.at[pl.ds(part * PART, PART), pl.ds(block * height, height)],
            arrived.at[block, part],
        )

    for block in range(row_blocks):
        for part in range(parts):
            fetch(block, part).start()

    depth = LANES * STRIP
    spread = (
        lax.broadcasted_iota(jnp.int32, (LANES, depth), 1) // STRIP
        == lax.broadcasted_iota(jnp.int32, (LANES, depth), 0)
    )
    spread = jnp.where(spread, 1.0, 0.0).astype(jnp.bfloat16)
    same = (
        lax.broadcasted_iota(jnp.int32, (STRIP, depth), 1) % STRIP
        == lax.broadcasted_iota(jnp.int32, (STRIP, depth), 0)
    )
    for v in range(blocks):
        shifted = shifted_ref[:, v, :].astype(jnp.bfloat16)
        wide = jnp.dot(shifted, spread, preferred_element_type=jnp.float32)
        for pair in range(walkers // 2):
            left[pair * 16:pair * 16 + 16, v * depth:(v + 1) * depth] = jnp.concatenate(
                [
                    jnp.where(same, jnp.broadcast_to(wide[w:w + 1], (STRIP, depth)), 0.0)
                    for w in (2 * pair, 2 * pair + 1)
                ],
                axis=0,
            ).astype(jnp.bfloat16)

    for block in range(row_blocks):
        for part in range(parts):
            fetch(block, part).wait()
            for strip in range(strips):
                top = block * height + strip * STRIP
                product = jnp.dot(
                    left[:, part * PART * STRIP:(part + 1) * PART * STRIP],
                    slab[part * PART:(part + 1) * PART, top:top + STRIP].reshape(PART * STRIP, columns),
                    preferred_element_type=jnp.float32,
                )
                if part == 0:
                    total[strip] = product
                else:
                    total[strip] += product
        for w in range(walkers):
            out_ref[w, block * height:(block + 1) * height] = jnp.concatenate(
                [total[strip, w * STRIP:(w + 1) * STRIP] for strip in range(strips)], axis=0
            ).astype(jnp.bfloat16)


def potential_rows(shifted, slab, rows):
    walkers, blocks, _ = shifted.shape
    vectors, _, columns = slab.shape
    height = min(16, rows)
    scratch = 2 * vectors * rows * columns + 2 * walkers * STRIP * (vectors * STRIP + 2 * (height // STRIP) * columns)
    return pl.pallas_call(
        potential_kernel,
        in_specs=[pl.BlockSpec(memory_space=pltpu.VMEM), pl.BlockSpec(memory_space=pl.ANY)],
        out_shape=jax.ShapeDtypeStruct((walkers, rows, columns), jnp.bfloat16),
        scratch_shapes=[
            pltpu.VMEM((vectors, rows, columns), slab.dtype),
            pltpu.VMEM((walkers * STRIP, vectors * STRIP), jnp.bfloat16),
            pltpu.VMEM((height // STRIP, walkers * STRIP, columns), jnp.float32),
            pltpu.SemaphoreType.DMA((rows // height, vectors // PART)),
        ],
        compiler_params=pltpu.CompilerParams(vmem_limit_bytes=scratch + 10 * MIB),
        cost_estimate=pl.CostEstimate(
            flops=2 * walkers * STRIP * rows * vectors * columns,
            bytes_accessed=2 * rows * vectors * columns,
            transcendentals=0,
        ),
    )(shifted, slab)


def taylor_kernel(blocks_ref, onebody_ref, walker_ref, out_ref, matrix, diagonal, terms):
    shares, kpoints, rows, size = blocks_ref.shape
    orbitals = size // kpoints
    columns = walker_ref.shape[1]
    per_tile = LANES // orbitals
    for k in range(kpoints):
        lanes = slice(k * orbitals, (k + 1) * orbitals)
        for tile in range(kpoints // per_tile):
            sources = [(k - tile * per_tile - i) % kpoints for i in range(per_tile)]
            for s in range(shares):
                top = k * orbitals + s * rows
                matrix[top:top + rows, tile * LANES:(tile + 1) * LANES] = jnp.concatenate(
                    [blocks_ref[s, q, :, lanes] for q in sources], axis=1
                )
    diagonal[...] = jnp.broadcast_to(onebody_ref[...], diagonal.shape)
    for order in range(1, TERMS):
        before = walker_ref if order == 1 else terms.at[order - 2]
        for first in range(0, kpoints, BAND):
            band = slice(first * orbitals, (first + BAND) * orbitals)
            product = jnp.dot(matrix[band], before[...], preferred_element_type=jnp.float32)
            here = before[band].astype(jnp.float32)
            product += jnp.concatenate([diagonal[band]] * (columns // LANES), axis=1) * here
            value = (product * (-1.0 / order)).astype(jnp.bfloat16)
            if order < TERMS - 1:
                terms[order - 1, band] = value
            else:
                total = walker_ref[band].astype(jnp.float32)
                for n in range(TERMS - 2):
                    total += terms[n, band].astype(jnp.float32)
                out_ref[band] = (total + value.astype(jnp.float32)).astype(jnp.bfloat16)


def taylor(blocks, onebody, walker):
    kpoints, orbitals = onebody.shape
    size, columns = walker.shape
    return pl.pallas_call(
        taylor_kernel,
        out_shape=jax.ShapeDtypeStruct(walker.shape, jnp.bfloat16),
        scratch_shapes=[
            pltpu.VMEM((size, size), jnp.bfloat16),
            pltpu.VMEM((size, LANES), jnp.float32),
            pltpu.VMEM((TERMS - 2, size, columns), jnp.bfloat16),
        ],
        compiler_params=pltpu.CompilerParams(vmem_limit_bytes=24 * MIB),
        cost_estimate=pl.CostEstimate(
            flops=2 * (TERMS - 1) * size * size * columns,
            bytes_accessed=2 * size * (size + 2 * columns),
            transcendentals=0,
        ),
    )(blocks, onebody.reshape(size, 1), walker)


def exchange(blocks, axes):
    return lax.all_to_all(blocks, axes, split_axis=0, concat_axis=0, tiled=True)


def per_device(fields, field_shift, cholesky, onebody, walkers):
    devices, groups = lax.axis_size("pb"), lax.axis_size("groups")
    local_walkers = fields.shape[0]
    kpoints, orbitals = onebody.shape
    vectors, rows_here, columns = cholesky.shape
    per_transfer = orbitals // rows_here

    shares = groups if local_walkers == 1 and per_transfer == 1 and rows_here % (16 * groups) == 0 else 1
    axes = ("groups", "pb") if shares > 1 else "pb"
    rows = rows_here // shares
    outgoing = [shift_fields(fields[w], field_shift, shares) for w in range(local_walkers)]
    outgoing = jnp.repeat(jnp.stack(outgoing, axis=2), per_transfer, axis=1)
    arrived = exchange(outgoing.reshape((shares * devices,) + outgoing.shape[2:]), axes)
    arrived = arrived.reshape((shares * devices * local_walkers,) + arrived.shape[2:])

    blocks = potential_rows(arrived, cholesky, rows)
    relayed = exchange(blocks.reshape(shares * devices, local_walkers, rows, columns), axes)
    results = [
        taylor(relayed[:, w].reshape(shares, kpoints, per_transfer * rows, columns), onebody, walkers[w])
        for w in range(local_walkers)
    ]
    return jnp.stack(results, axis=0)


def solution(mesh):
    return jax.shard_map(
        per_device,
        mesh=mesh,
        in_specs=(
            P(("groups", "pb"), None, None),
            P(),
            P(None, "pb", None),
            P(),
            P(("groups", "pb"), None, None),
        ),
        out_specs=P(("groups", "pb"), None, None),
        check_vma=False,
    )
```

```python
import functools

import jax
import jax.numpy as jnp
from jax import lax
from jax.experimental import pallas as pl
from jax.experimental.pallas import tpu as pltpu
from jax.sharding import PartitionSpec as P

TERMS = 6
LANES = 128
STRIP = 8
PART = 128
BAND = 4
MIB = 1024 * 1024


def shift_kernel(fields_ref, shift_ref, out_ref, fields, shift, arrived):
    copies = [
        pltpu.make_async_copy(fields_ref, fields, arrived.at[0]),
        pltpu.make_async_copy(shift_ref, shift, arrived.at[1]),
    ]
    for copy in copies:
        copy.start()
    for copy in copies:
        copy.wait()
    shifted = (fields[...] + shift[...]).astype(jnp.bfloat16).astype(jnp.float32)
    for copy in range(out_ref.shape[0]):
        for v in range(out_ref.shape[2]):
            out_ref[copy, :, v, :] = shifted[:, v * LANES:(v + 1) * LANES]


def shift_fields(fields, field_shift, copies):
    kpoints, vectors = field_shift.shape
    return pl.pallas_call(
        shift_kernel,
        in_specs=[pl.BlockSpec(memory_space=pltpu.HBM)] * 2,
        out_shape=jax.ShapeDtypeStruct((copies, kpoints, vectors // LANES, LANES), jnp.float32),
        scratch_shapes=[
            pltpu.VMEM(fields.shape, jnp.float32),
            pltpu.VMEM(field_shift.shape, jnp.float32),
            pltpu.SemaphoreType.DMA((2,)),
        ],
        compiler_params=pltpu.CompilerParams(vmem_limit_bytes=8 * MIB),
    )(*[pltpu.with_memory_space_constraint(array, pltpu.HBM) for array in (fields, field_shift)])


def slab_steps(vectors, rows, height):
    steps = []
    for top in range(0, rows, height):
        last = [PART // 2, PART // 4, PART // 4] if top + height == rows else [PART]
        sizes = [PART] * (vectors // PART - 1) + last
        steps += [(top, sum(sizes[:i]), size) for i, size in enumerate(sizes)]
    return steps


def share_top(groups, rows):
    return 0 if groups == 1 else pl.multiple_of(lax.axis_index("groups") * rows, rows)


def potential_kernel(groups, steps, shifted_ref, slab_ref, out_ref, slab, left, total, arrived):
    walkers, blocks, _ = shifted_ref.shape
    vectors, rows, columns = slab.shape
    strips = total.shape[0]
    height = strips * STRIP
    first = share_top(groups, rows)

    def fetch(step):
        top, vector, count = steps[step]
        return pltpu.make_async_copy(
            slab_ref.at[pl.ds(vector, count), pl.ds(first + top, height)],
            slab.at[pl.ds(vector, count), pl.ds(top, height)],
            arrived.at[step],
        )

    for step in range(len(steps)):
        fetch(step).start()

    depth = LANES * STRIP
    spread = (
        lax.broadcasted_iota(jnp.int32, (LANES, depth), 1) // STRIP
        == lax.broadcasted_iota(jnp.int32, (LANES, depth), 0)
    )
    spread = jnp.where(spread, 1.0, 0.0).astype(jnp.bfloat16)
    same = (
        lax.broadcasted_iota(jnp.int32, (STRIP, depth), 1) % STRIP
        == lax.broadcasted_iota(jnp.int32, (STRIP, depth), 0)
    )
    for v in range(blocks):
        shifted = shifted_ref[:, v, :].astype(jnp.bfloat16)
        wide = jnp.dot(shifted, spread, preferred_element_type=jnp.float32)
        for pair in range(walkers // 2):
            left[pair * 16:pair * 16 + 16, v * depth:(v + 1) * depth] = jnp.concatenate(
                [
                    jnp.where(same, jnp.broadcast_to(wide[w:w + 1], (STRIP, depth)), 0.0)
                    for w in (2 * pair, 2 * pair + 1)
                ],
                axis=0,
            ).astype(jnp.bfloat16)

    for step, (top, vector, count) in enumerate(steps):
        fetch(step).wait()
        for strip in range(strips):
            start = top + strip * STRIP
            product = jnp.dot(
                left[:, vector * STRIP:(vector + count) * STRIP],
                slab[vector:vector + count, start:start + STRIP].reshape(count * STRIP, columns),
                preferred_element_type=jnp.float32,
            )
            if vector == 0:
                total[strip] = product
            else:
                total[strip] += product
        if vector + count == vectors:
            for w in range(walkers):
                out_ref[w, top:top + height] = jnp.concatenate(
                    [total[strip, w * STRIP:(w + 1) * STRIP] for strip in range(strips)], axis=0
                ).astype(jnp.bfloat16)


def potential_rows(shifted, slab, rows):
    walkers, blocks, _ = shifted.shape
    vectors, rows_here, columns = slab.shape
    height = min(16, rows)
    steps = slab_steps(vectors, rows, height)
    scratch = 2 * vectors * rows * columns + 2 * walkers * STRIP * (vectors * STRIP + 2 * (height // STRIP) * columns)
    return pl.pallas_call(
        functools.partial(potential_kernel, rows_here // rows, steps),
        in_specs=[pl.BlockSpec(memory_space=pltpu.VMEM), pl.BlockSpec(memory_space=pl.ANY)],
        out_shape=jax.ShapeDtypeStruct((walkers, rows, columns), jnp.bfloat16),
        scratch_shapes=[
            pltpu.VMEM((vectors, rows, columns), slab.dtype),
            pltpu.VMEM((walkers * STRIP, vectors * STRIP), jnp.bfloat16),
            pltpu.VMEM((height // STRIP, walkers * STRIP, columns), jnp.float32),
            pltpu.SemaphoreType.DMA((len(steps),)),
        ],
        compiler_params=pltpu.CompilerParams(vmem_limit_bytes=scratch + 8 * MIB),
        cost_estimate=pl.CostEstimate(
            flops=2 * walkers * STRIP * rows * vectors * columns,
            bytes_accessed=2 * rows * vectors * columns,
            transcendentals=0,
        ),
    )(shifted, slab)


def taylor_kernel(blocks_ref, onebody_ref, walker_ref, out_ref, matrix, diagonal, terms, result, sent):
    shares, kpoints, rows, size = blocks_ref.shape
    orbitals = size // kpoints
    columns = walker_ref.shape[1]
    per_tile = LANES // orbitals
    own = (
        lax.broadcasted_iota(jnp.int32, (orbitals, orbitals), 0)
        == lax.broadcasted_iota(jnp.int32, (orbitals, orbitals), 1)
    )

    def arrange(k):
        lanes = slice(k * orbitals, (k + 1) * orbitals)
        for tile in range(kpoints // per_tile):
            sources = [(k - tile * per_tile - i) % kpoints for i in range(per_tile)]
            for s in range(shares):
                top = k * orbitals + s * rows
                matrix[top:top + rows, tile * LANES:(tile + 1) * LANES] = jnp.concatenate(
                    [blocks_ref[s, q, :, lanes] for q in sources], axis=1
                )
        column = jnp.sum(jnp.where(own, onebody_ref[k:k + 1], 0.0), axis=1, keepdims=True)
        diagonal[lanes] = jnp.broadcast_to(column, (orbitals, LANES))

    def send(first):
        band = pl.ds(first * orbitals, BAND * orbitals)
        return pltpu.make_async_copy(result.at[band], out_ref.at[band], sent.at[first // BAND])

    for order in range(1, TERMS):
        before = walker_ref if order == 1 else terms.at[order - 2]
        for first in range(0, kpoints, BAND):
            band = slice(first * orbitals, (first + BAND) * orbitals)
            if order == 1:
                for k in range(first, first + BAND):
                    arrange(k)
            product = jnp.dot(matrix[band], before[...], preferred_element_type=jnp.float32)
            here = before[band].astype(jnp.float32)
            product += jnp.concatenate([diagonal[band]] * (columns // LANES), axis=1) * here
            value = (product * (-1.0 / order)).astype(jnp.bfloat16)
            if order < TERMS - 1:
                terms[order - 1, band] = value
            else:
                total = walker_ref[band].astype(jnp.float32)
                for n in range(TERMS - 2):
                    total += terms[n, band].astype(jnp.float32)
                result[band] = (total + value.astype(jnp.float32)).astype(jnp.bfloat16)
                send(first).start()
    for first in range(0, kpoints, BAND):
        send(first).wait()


def taylor(blocks, onebody, walker):
    kpoints, _ = onebody.shape
    size, columns = walker.shape
    return pl.pallas_call(
        taylor_kernel,
        out_specs=pl.BlockSpec(memory_space=pl.ANY),
        out_shape=jax.ShapeDtypeStruct(walker.shape, jnp.bfloat16),
        scratch_shapes=[
            pltpu.VMEM((size, size), jnp.bfloat16),
            pltpu.VMEM((size, LANES), jnp.float32),
            pltpu.VMEM((TERMS - 2, size, columns), jnp.bfloat16),
            pltpu.VMEM((size, columns), jnp.bfloat16),
            pltpu.SemaphoreType.DMA((kpoints // BAND,)),
        ],
        compiler_params=pltpu.CompilerParams(vmem_limit_bytes=24 * MIB),
        cost_estimate=pl.CostEstimate(
            flops=2 * (TERMS - 1) * size * size * columns,
            bytes_accessed=2 * size * (size + 2 * columns),
            transcendentals=0,
        ),
    )(blocks, onebody, walker)


def exchange(blocks, axes):
    return lax.all_to_all(blocks, axes, split_axis=0, concat_axis=0, tiled=True)


def per_device(fields, field_shift, cholesky, onebody, walkers):
    devices, groups = lax.axis_size("pb"), lax.axis_size("groups")
    local_walkers = fields.shape[0]
    kpoints, orbitals = onebody.shape
    vectors, rows_here, columns = cholesky.shape
    per_transfer = orbitals // rows_here

    shares = groups if local_walkers == 1 and per_transfer == 1 and rows_here % (16 * groups) == 0 else 1
    axes = ("groups", "pb") if shares > 1 else "pb"
    rows = rows_here // shares
    outgoing = [shift_fields(fields[w], field_shift, shares) for w in range(local_walkers)]
    outgoing = jnp.repeat(jnp.stack(outgoing, axis=2), per_transfer, axis=1)
    arrived = exchange(outgoing.reshape((shares * devices,) + outgoing.shape[2:]), axes)
    arrived = arrived.reshape((shares * devices * local_walkers,) + arrived.shape[2:])

    blocks = potential_rows(arrived, cholesky, rows)
    relayed = exchange(blocks.reshape(shares * devices, local_walkers, rows, columns), axes)
    results = [
        taylor(relayed[:, w].reshape(shares, kpoints, per_transfer * rows, columns), onebody, walkers[w])
        for w in range(local_walkers)
    ]
    return jnp.stack(results, axis=0)


def solution(mesh):
    return jax.shard_map(
        per_device,
        mesh=mesh,
        in_specs=(
            P(("groups", "pb"), None, None),
            P(),
            P(None, "pb", None),
            P(),
            P(("groups", "pb"), None, None),
        ),
        out_specs=P(("groups", "pb"), None, None),
        check_vma=False,
    )
```

```python
import functools

import jax
import jax.numpy as jnp
from jax import lax
from jax.experimental import pallas as pl
from jax.experimental.pallas import tpu as pltpu
from jax.sharding import PartitionSpec as P

TERMS = 6
LANES = 128
STRIP = 8
PART = 128
BAND = 4
MIB = 1024 * 1024


def shift_kernel(fields_ref, shift_ref, out_ref, fields, shift, arrived):
    copies = [
        pltpu.make_async_copy(fields_ref, fields, arrived.at[0]),
        pltpu.make_async_copy(shift_ref, shift, arrived.at[1]),
    ]
    for copy in copies:
        copy.start()
    for copy in copies:
        copy.wait()
    shifted = (fields[...] + shift[...]).astype(jnp.bfloat16).astype(jnp.float32)
    for copy in range(out_ref.shape[1]):
        for v in range(out_ref.shape[2]):
            out_ref[:, copy, v, :] = shifted[:, v * LANES:(v + 1) * LANES]


def shift_fields(fields, field_shift, copies):
    kpoints, vectors = field_shift.shape
    return pl.pallas_call(
        shift_kernel,
        in_specs=[pl.BlockSpec(memory_space=pltpu.HBM)] * 2,
        out_shape=jax.ShapeDtypeStruct((kpoints, copies, vectors // LANES, LANES), jnp.float32),
        scratch_shapes=[
            pltpu.VMEM(fields.shape, jnp.float32),
            pltpu.VMEM(field_shift.shape, jnp.float32),
            pltpu.SemaphoreType.DMA((2,)),
        ],
        compiler_params=pltpu.CompilerParams(vmem_limit_bytes=8 * MIB),
    )(*[pltpu.with_memory_space_constraint(array, pltpu.HBM) for array in (fields, field_shift)])


def slab_steps(vectors, rows, height):
    steps = []
    for top in range(0, rows, height):
        last = [PART // 2, PART // 4, PART // 4] if top + height == rows else [PART]
        sizes = [PART] * (vectors // PART - 1) + last
        steps += [(top, sum(sizes[:i]), size) for i, size in enumerate(sizes)]
    return steps


def share_top(groups, rows):
    return 0 if groups == 1 else pl.multiple_of(lax.axis_index("groups") * rows, rows)


def potential_kernel(groups, steps, shifted_ref, slab_ref, out_ref, slab, left, total, arrived):
    walkers, blocks, _ = shifted_ref.shape
    vectors, rows, columns = slab.shape
    strips = total.shape[0]
    height = strips * STRIP
    first = share_top(groups, rows)

    def fetch(step):
        top, vector, count = steps[step]
        return pltpu.make_async_copy(
            slab_ref.at[pl.ds(vector, count), pl.ds(first + top, height)],
            slab.at[pl.ds(vector, count), pl.ds(top, height)],
            arrived.at[step],
        )

    for step in range(len(steps)):
        fetch(step).start()

    depth = LANES * STRIP
    spread = (
        lax.broadcasted_iota(jnp.int32, (LANES, depth), 1) // STRIP
        == lax.broadcasted_iota(jnp.int32, (LANES, depth), 0)
    )
    spread = jnp.where(spread, 1.0, 0.0).astype(jnp.bfloat16)
    same = (
        lax.broadcasted_iota(jnp.int32, (STRIP, depth), 1) % STRIP
        == lax.broadcasted_iota(jnp.int32, (STRIP, depth), 0)
    )
    for v in range(blocks):
        shifted = shifted_ref[:, v, :].astype(jnp.bfloat16)
        wide = jnp.dot(shifted, spread, preferred_element_type=jnp.float32)
        for pair in range(walkers // 2):
            left[pair * 16:pair * 16 + 16, v * depth:(v + 1) * depth] = jnp.concatenate(
                [
                    jnp.where(same, jnp.broadcast_to(wide[w:w + 1], (STRIP, depth)), 0.0)
                    for w in (2 * pair, 2 * pair + 1)
                ],
                axis=0,
            ).astype(jnp.bfloat16)

    for step, (top, vector, count) in enumerate(steps):
        fetch(step).wait()
        for strip in range(strips):
            start = top + strip * STRIP
            product = jnp.dot(
                left[:, vector * STRIP:(vector + count) * STRIP],
                slab[vector:vector + count, start:start + STRIP].reshape(count * STRIP, columns),
                preferred_element_type=jnp.float32,
            )
            if vector == 0:
                total[strip] = product
            else:
                total[strip] += product
        if vector + count == vectors:
            for w in range(walkers):
                out_ref[w, top:top + height] = jnp.concatenate(
                    [total[strip, w * STRIP:(w + 1) * STRIP] for strip in range(strips)], axis=0
                ).astype(jnp.bfloat16)


def potential_rows(shifted, slab, rows):
    walkers, blocks, _ = shifted.shape
    vectors, rows_here, columns = slab.shape
    height = min(16, rows)
    steps = slab_steps(vectors, rows, height)
    scratch = 2 * vectors * rows * columns + 2 * walkers * STRIP * (vectors * STRIP + 2 * (height // STRIP) * columns)
    return pl.pallas_call(
        functools.partial(potential_kernel, rows_here // rows, steps),
        in_specs=[pl.BlockSpec(memory_space=pltpu.VMEM), pl.BlockSpec(memory_space=pl.ANY)],
        out_shape=jax.ShapeDtypeStruct((walkers, rows, columns), jnp.bfloat16),
        scratch_shapes=[
            pltpu.VMEM((vectors, rows, columns), slab.dtype),
            pltpu.VMEM((walkers * STRIP, vectors * STRIP), jnp.bfloat16),
            pltpu.VMEM((height // STRIP, walkers * STRIP, columns), jnp.float32),
            pltpu.SemaphoreType.DMA((len(steps),)),
        ],
        compiler_params=pltpu.CompilerParams(vmem_limit_bytes=scratch + 8 * MIB),
        cost_estimate=pl.CostEstimate(
            flops=2 * walkers * STRIP * rows * vectors * columns,
            bytes_accessed=2 * rows * vectors * columns,
            transcendentals=0,
        ),
    )(shifted, slab)


def taylor_kernel(blocks_ref, onebody_ref, walker_ref, out_ref, matrix, diagonal, terms, result, sent):
    kpoints, shares, rows, size = blocks_ref.shape
    orbitals = size // kpoints
    columns = walker_ref.shape[1]
    per_tile = LANES // orbitals
    own = (
        lax.broadcasted_iota(jnp.int32, (orbitals, orbitals), 0)
        == lax.broadcasted_iota(jnp.int32, (orbitals, orbitals), 1)
    )

    def arrange(k):
        lanes = slice(k * orbitals, (k + 1) * orbitals)
        for tile in range(kpoints // per_tile):
            sources = [(k - tile * per_tile - i) % kpoints for i in range(per_tile)]
            for s in range(shares):
                top = k * orbitals + s * rows
                matrix[top:top + rows, tile * LANES:(tile + 1) * LANES] = jnp.concatenate(
                    [blocks_ref[q, s, :, lanes] for q in sources], axis=1
                )
        column = jnp.sum(jnp.where(own, onebody_ref[k:k + 1], 0.0), axis=1, keepdims=True)
        diagonal[lanes] = jnp.broadcast_to(column, (orbitals, LANES))

    def send(first):
        band = pl.ds(first * orbitals, BAND * orbitals)
        return pltpu.make_async_copy(result.at[band], out_ref.at[band], sent.at[first // BAND])

    for order in range(1, TERMS):
        before = walker_ref if order == 1 else terms.at[order - 2]
        for first in range(0, kpoints, BAND):
            band = slice(first * orbitals, (first + BAND) * orbitals)
            if order == 1:
                for k in range(first, first + BAND):
                    arrange(k)
            product = jnp.dot(matrix[band], before[...], preferred_element_type=jnp.float32)
            here = before[band].astype(jnp.float32)
            product += jnp.concatenate([diagonal[band]] * (columns // LANES), axis=1) * here
            value = (product * (-1.0 / order)).astype(jnp.bfloat16)
            if order < TERMS - 1:
                terms[order - 1, band] = value
            else:
                total = walker_ref[band].astype(jnp.float32)
                for n in range(TERMS - 2):
                    total += terms[n, band].astype(jnp.float32)
                result[band] = (total + value.astype(jnp.float32)).astype(jnp.bfloat16)
                send(first).start()
    for first in range(0, kpoints, BAND):
        send(first).wait()


def taylor(blocks, onebody, walker):
    kpoints, _ = onebody.shape
    size, columns = walker.shape
    return pl.pallas_call(
        taylor_kernel,
        out_specs=pl.BlockSpec(memory_space=pl.ANY),
        out_shape=jax.ShapeDtypeStruct(walker.shape, jnp.bfloat16),
        scratch_shapes=[
            pltpu.VMEM((size, size), jnp.bfloat16),
            pltpu.VMEM((size, LANES), jnp.float32),
            pltpu.VMEM((TERMS - 2, size, columns), jnp.bfloat16),
            pltpu.VMEM((size, columns), jnp.bfloat16),
            pltpu.SemaphoreType.DMA((kpoints // BAND,)),
        ],
        compiler_params=pltpu.CompilerParams(vmem_limit_bytes=24 * MIB),
        cost_estimate=pl.CostEstimate(
            flops=2 * (TERMS - 1) * size * size * columns,
            bytes_accessed=2 * size * (size + 2 * columns),
            transcendentals=0,
        ),
    )(blocks, onebody, walker)


def exchange(blocks, axes):
    return lax.all_to_all(blocks, axes, split_axis=0, concat_axis=0, tiled=True)


def per_device(fields, field_shift, cholesky, onebody, walkers):
    devices, groups = lax.axis_size("pb"), lax.axis_size("groups")
    local_walkers = fields.shape[0]
    kpoints, orbitals = onebody.shape
    vectors, rows_here, columns = cholesky.shape
    per_transfer = orbitals // rows_here

    shares = groups if local_walkers == 1 and per_transfer == 1 and rows_here % (16 * groups) == 0 else 1
    axes = ("pb", "groups") if shares > 1 else "pb"
    rows = rows_here // shares
    outgoing = [shift_fields(fields[w], field_shift, shares) for w in range(local_walkers)]
    outgoing = jnp.repeat(jnp.stack(outgoing, axis=2), per_transfer, axis=0)
    arrived = exchange(outgoing.reshape((devices * shares,) + outgoing.shape[2:]), axes)
    arrived = arrived.reshape((devices * shares * local_walkers,) + arrived.shape[2:])

    blocks = potential_rows(arrived, cholesky, rows)
    relayed = exchange(blocks.reshape(devices * shares, local_walkers, rows, columns), axes)
    results = [
        taylor(relayed[:, w].reshape(kpoints, shares, per_transfer * rows, columns), onebody, walkers[w])
        for w in range(local_walkers)
    ]
    return jnp.stack(results, axis=0)


def solution(mesh):
    return jax.shard_map(
        per_device,
        mesh=mesh,
        in_specs=(
            P(("groups", "pb"), None, None),
            P(),
            P(None, "pb", None),
            P(),
            P(("groups", "pb"), None, None),
        ),
        out_specs=P(("groups", "pb"), None, None),
        check_vma=False,
    )
```

```python
import functools

import jax
import jax.numpy as jnp
from jax import lax
from jax.experimental import pallas as pl
from jax.experimental.pallas import tpu as pltpu
from jax.sharding import PartitionSpec as P

TERMS = 6
LANES = 128
STRIP = 8
PART = 64
BAND = 4
MIB = 1024 * 1024


def shift_kernel(fields_ref, shift_ref, out_ref, fields, shift, spread, arrived):
    copies = [
        pltpu.make_async_copy(fields_ref, fields, arrived.at[0]),
        pltpu.make_async_copy(shift_ref, shift, arrived.at[1]),
    ]
    for copy in copies:
        copy.start()
    for copy in copies:
        copy.wait()
    shifted = (fields[...] + shift[...]).astype(jnp.bfloat16)
    for copy in range(out_ref.shape[1]):
        for v in range(out_ref.shape[2]):
            spread[:, copy, v, :] = shifted[:, v * LANES:(v + 1) * LANES].astype(jnp.float32)
    out_ref[...] = spread[...].astype(jnp.bfloat16)


def shift_fields(fields, field_shift, copies):
    kpoints, vectors = field_shift.shape
    return pl.pallas_call(
        shift_kernel,
        in_specs=[pl.BlockSpec(memory_space=pltpu.HBM)] * 2,
        out_shape=jax.ShapeDtypeStruct((kpoints, copies, vectors // LANES, LANES), jnp.bfloat16),
        scratch_shapes=[
            pltpu.VMEM(fields.shape, jnp.float32),
            pltpu.VMEM(field_shift.shape, jnp.float32),
            pltpu.VMEM((kpoints, copies, vectors // LANES, LANES), jnp.float32),
            pltpu.SemaphoreType.DMA((2,)),
        ],
        compiler_params=pltpu.CompilerParams(vmem_limit_bytes=8 * MIB),
    )(*[pltpu.with_memory_space_constraint(array, pltpu.HBM) for array in (fields, field_shift)])


def slab_steps(vectors, rows, height):
    steps = []
    for top in range(0, rows, height):
        last = [PART // 2, PART // 2] if top + height == rows else [PART]
        sizes = [PART] * (vectors // PART - 1) + last
        steps += [(top, sum(sizes[:i]), size) for i, size in enumerate(sizes)]
    return steps


def share_top(groups, rows):
    return 0 if groups == 1 else pl.multiple_of(lax.axis_index("groups") * rows, rows)


def potential_kernel(groups, steps, shifted_ref, slab_ref, out_ref, slab, fields, left, total, arrived):
    walkers, blocks, _ = shifted_ref.shape
    vectors, rows, columns = slab.shape
    strips = total.shape[0]
    height = strips * STRIP
    first = share_top(groups, rows)

    def fetch(step):
        top, vector, count = steps[step]
        return pltpu.make_async_copy(
            slab_ref.at[pl.ds(vector, count), pl.ds(first + top, height)],
            slab.at[pl.ds(vector, count), pl.ds(top, height)],
            arrived.at[step],
        )

    for step in range(len(steps)):
        fetch(step).start()

    depth = LANES * STRIP
    spread = (
        lax.broadcasted_iota(jnp.int32, (LANES, depth), 1) // STRIP
        == lax.broadcasted_iota(jnp.int32, (LANES, depth), 0)
    )
    spread = jnp.where(spread, 1.0, 0.0).astype(jnp.bfloat16)
    same = (
        lax.broadcasted_iota(jnp.int32, (STRIP, depth), 1) % STRIP
        == lax.broadcasted_iota(jnp.int32, (STRIP, depth), 0)
    )
    fields[...] = shifted_ref[...].astype(jnp.float32)
    for v in range(blocks):
        shifted = fields[:, v, :].astype(jnp.bfloat16)
        wide = jnp.dot(shifted, spread, preferred_element_type=jnp.float32)
        for pair in range(walkers // 2):
            left[pair * 16:pair * 16 + 16, v * depth:(v + 1) * depth] = jnp.concatenate(
                [
                    jnp.where(same, jnp.broadcast_to(wide[w:w + 1], (STRIP, depth)), 0.0)
                    for w in (2 * pair, 2 * pair + 1)
                ],
                axis=0,
            ).astype(jnp.bfloat16)

    for step, (top, vector, count) in enumerate(steps):
        fetch(step).wait()
        for strip in range(strips):
            start = top + strip * STRIP
            product = jnp.dot(
                left[:, vector * STRIP:(vector + count) * STRIP],
                slab[vector:vector + count, start:start + STRIP].reshape(count * STRIP, columns),
                preferred_element_type=jnp.float32,
            )
            if vector == 0:
                total[strip] = product
            else:
                total[strip] += product
        if vector + count == vectors:
            for w in range(walkers):
                out_ref[w, top:top + height] = jnp.concatenate(
                    [total[strip, w * STRIP:(w + 1) * STRIP] for strip in range(strips)], axis=0
                ).astype(jnp.bfloat16)


def potential_rows(shifted, slab, rows):
    walkers, blocks, _ = shifted.shape
    vectors, rows_here, columns = slab.shape
    height = min(16, rows)
    steps = slab_steps(vectors, rows, height)
    scratch = 2 * vectors * rows * columns + 2 * walkers * STRIP * (vectors * STRIP + 2 * (height // STRIP) * columns)
    return pl.pallas_call(
        functools.partial(potential_kernel, rows_here // rows, steps),
        in_specs=[pl.BlockSpec(memory_space=pltpu.VMEM), pl.BlockSpec(memory_space=pl.ANY)],
        out_shape=jax.ShapeDtypeStruct((walkers, rows, columns), jnp.bfloat16),
        scratch_shapes=[
            pltpu.VMEM((vectors, rows, columns), slab.dtype),
            pltpu.VMEM(shifted.shape, jnp.float32),
            pltpu.VMEM((walkers * STRIP, vectors * STRIP), jnp.bfloat16),
            pltpu.VMEM((height // STRIP, walkers * STRIP, columns), jnp.float32),
            pltpu.SemaphoreType.DMA((len(steps),)),
        ],
        compiler_params=pltpu.CompilerParams(vmem_limit_bytes=scratch + (8 if rows < rows_here else 24) * MIB),
        cost_estimate=pl.CostEstimate(
            flops=2 * walkers * STRIP * rows * vectors * columns,
            bytes_accessed=2 * rows * vectors * columns,
            transcendentals=0,
        ),
    )(shifted, slab)


def taylor_kernel(blocks_ref, onebody_ref, walker_ref, out_ref, matrix, diagonal, terms, result, sent):
    kpoints, shares, rows, size = blocks_ref.shape
    orbitals = size // kpoints
    columns = walker_ref.shape[1]
    per_tile = LANES // orbitals
    own = (
        lax.broadcasted_iota(jnp.int32, (orbitals, orbitals), 0)
        == lax.broadcasted_iota(jnp.int32, (orbitals, orbitals), 1)
    )

    def arrange(k):
        lanes = slice(k * orbitals, (k + 1) * orbitals)
        for tile in range(kpoints // per_tile):
            sources = [(k - tile * per_tile - i) % kpoints for i in range(per_tile)]
            for s in range(shares):
                top = k * orbitals + s * rows
                matrix[top:top + rows, tile * LANES:(tile + 1) * LANES] = jnp.concatenate(
                    [blocks_ref[q, s, :, lanes] for q in sources], axis=1
                )
        column = jnp.sum(jnp.where(own, onebody_ref[k:k + 1], 0.0), axis=1, keepdims=True)
        diagonal[lanes] = jnp.broadcast_to(column, (orbitals, LANES))

    def send(first):
        band = pl.ds(first * orbitals, BAND * orbitals)
        return pltpu.make_async_copy(result.at[band], out_ref.at[band], sent.at[first // BAND])

    for order in range(1, TERMS):
        before = walker_ref if order == 1 else terms.at[order - 2]
        for first in range(0, kpoints, BAND):
            band = slice(first * orbitals, (first + BAND) * orbitals)
            if order == 1:
                for k in range(first, first + BAND):
                    arrange(k)
            product = jnp.dot(matrix[band], before[...], preferred_element_type=jnp.float32)
            here = before[band].astype(jnp.float32)
            product += jnp.concatenate([diagonal[band]] * (columns // LANES), axis=1) * here
            value = (product * (-1.0 / order)).astype(jnp.bfloat16)
            if order < TERMS - 1:
                terms[order - 1, band] = value
            else:
                total = walker_ref[band].astype(jnp.float32)
                for n in range(TERMS - 2):
                    total += terms[n, band].astype(jnp.float32)
                result[band] = (total + value.astype(jnp.float32)).astype(jnp.bfloat16)
                send(first).start()
    for first in range(0, kpoints, BAND):
        send(first).wait()


def taylor(blocks, onebody, walker):
    kpoints, _ = onebody.shape
    size, columns = walker.shape
    return pl.pallas_call(
        taylor_kernel,
        out_specs=pl.BlockSpec(memory_space=pl.ANY),
        out_shape=jax.ShapeDtypeStruct(walker.shape, jnp.bfloat16),
        scratch_shapes=[
            pltpu.VMEM((size, size), jnp.bfloat16),
            pltpu.VMEM((size, LANES), jnp.float32),
            pltpu.VMEM((TERMS - 2, size, columns), jnp.bfloat16),
            pltpu.VMEM((size, columns), jnp.bfloat16),
            pltpu.SemaphoreType.DMA((kpoints // BAND,)),
        ],
        compiler_params=pltpu.CompilerParams(vmem_limit_bytes=24 * MIB),
        cost_estimate=pl.CostEstimate(
            flops=2 * (TERMS - 1) * size * size * columns,
            bytes_accessed=2 * size * (size + 2 * columns),
            transcendentals=0,
        ),
    )(blocks, onebody, walker)


def exchange(blocks, axes):
    return lax.all_to_all(blocks, axes, split_axis=0, concat_axis=0, tiled=True)


def per_device(fields, field_shift, cholesky, onebody, walkers):
    devices, groups = lax.axis_size("pb"), lax.axis_size("groups")
    local_walkers = fields.shape[0]
    kpoints, orbitals = onebody.shape
    vectors, rows_here, columns = cholesky.shape
    per_transfer = orbitals // rows_here

    shares = groups if local_walkers == 1 and per_transfer == 1 and rows_here % (16 * groups) == 0 else 1
    axes = ("pb", "groups") if shares > 1 else "pb"
    rows = rows_here // shares
    outgoing = [shift_fields(fields[w], field_shift, shares) for w in range(local_walkers)]
    outgoing = jnp.repeat(jnp.stack(outgoing, axis=2), per_transfer, axis=0)
    arrived = exchange(outgoing.reshape((devices * shares,) + outgoing.shape[2:]), axes)
    arrived = arrived.reshape((devices * shares * local_walkers,) + arrived.shape[2:])

    blocks = potential_rows(arrived, cholesky, rows)
    relayed = exchange(blocks.reshape(devices * shares, local_walkers, rows, columns), axes)
    results = [
        taylor(relayed[:, w].reshape(kpoints, shares, per_transfer * rows, columns), onebody, walkers[w])
        for w in range(local_walkers)
    ]
    return jnp.stack(results, axis=0)


def solution(mesh):
    return jax.shard_map(
        per_device,
        mesh=mesh,
        in_specs=(
            P(("groups", "pb"), None, None),
            P(),
            P(None, "pb", None),
            P(),
            P(("groups", "pb"), None, None),
        ),
        out_specs=P(("groups", "pb"), None, None),
        check_vma=False,
    )
```

```python
import functools

import jax
import jax.numpy as jnp
from jax import lax
from jax.experimental import pallas as pl
from jax.experimental.pallas import tpu as pltpu
from jax.sharding import PartitionSpec as P

TERMS = 6
LANES = 128
STRIP = 8
PART = 64
BAND = 4
MIB = 1024 * 1024


def shift_kernel(fields_ref, shift_ref, out_ref, fields, shift, spread, arrived):
    copies = [
        pltpu.make_async_copy(fields_ref, fields, arrived.at[0]),
        pltpu.make_async_copy(shift_ref, shift, arrived.at[1]),
    ]
    for copy in copies:
        copy.start()
    for copy in copies:
        copy.wait()
    shifted = (fields[...] + shift[...]).astype(jnp.bfloat16)
    for copy in range(out_ref.shape[1]):
        for v in range(out_ref.shape[2]):
            spread[:, copy, v, :] = shifted[:, v * LANES:(v + 1) * LANES].astype(jnp.float32)
    out_ref[...] = spread[...].astype(jnp.bfloat16)


def shift_fields(fields, field_shift, copies):
    kpoints, vectors = field_shift.shape
    return pl.pallas_call(
        shift_kernel,
        in_specs=[pl.BlockSpec(memory_space=pltpu.HBM)] * 2,
        out_shape=jax.ShapeDtypeStruct((kpoints, copies, vectors // LANES, LANES), jnp.bfloat16),
        scratch_shapes=[
            pltpu.VMEM(fields.shape, jnp.float32),
            pltpu.VMEM(field_shift.shape, jnp.float32),
            pltpu.VMEM((kpoints, copies, vectors // LANES, LANES), jnp.float32),
            pltpu.SemaphoreType.DMA((2,)),
        ],
        compiler_params=pltpu.CompilerParams(vmem_limit_bytes=8 * MIB),
    )(*[pltpu.with_memory_space_constraint(array, pltpu.HBM) for array in (fields, field_shift)])


def slab_steps(vectors, rows, height):
    steps = []
    for top in range(0, rows, height):
        last = [PART // 2, PART // 2] if top + height == rows else [PART]
        sizes = [PART] * (vectors // PART - 1) + last
        steps += [(top, sum(sizes[:i]), size) for i, size in enumerate(sizes)]
    return steps


def share_top(groups, rows):
    return 0 if groups == 1 else pl.multiple_of(lax.axis_index("groups") * rows, rows)


def potential_kernel(groups, steps, shifted_ref, slab_ref, out_ref, slab, fields, left, total, arrived):
    walkers, blocks, _ = shifted_ref.shape
    vectors, rows, columns = slab.shape
    strips = total.shape[0]
    height = strips * STRIP
    first = share_top(groups, rows)

    def fetch(step):
        top, vector, count = steps[step]
        return pltpu.make_async_copy(
            slab_ref.at[pl.ds(vector, count), pl.ds(first + top, height)],
            slab.at[pl.ds(vector, count), pl.ds(top, height)],
            arrived.at[step],
        )

    for step in range(len(steps)):
        fetch(step).start()

    depth = LANES * STRIP
    spread = (
        lax.broadcasted_iota(jnp.int32, (LANES, depth), 1) // STRIP
        == lax.broadcasted_iota(jnp.int32, (LANES, depth), 0)
    )
    spread = jnp.where(spread, 1.0, 0.0).astype(jnp.bfloat16)
    same = (
        lax.broadcasted_iota(jnp.int32, (STRIP, depth), 1) % STRIP
        == lax.broadcasted_iota(jnp.int32, (STRIP, depth), 0)
    )
    fields[...] = shifted_ref[...].astype(jnp.float32)
    for v in range(blocks):
        shifted = fields[:, v, :].astype(jnp.bfloat16)
        wide = jnp.dot(shifted, spread, preferred_element_type=jnp.float32)
        for pair in range(walkers // 2):
            left[pair * 16:pair * 16 + 16, v * depth:(v + 1) * depth] = jnp.concatenate(
                [
                    jnp.where(same, jnp.broadcast_to(wide[w:w + 1], (STRIP, depth)), 0.0)
                    for w in (2 * pair, 2 * pair + 1)
                ],
                axis=0,
            ).astype(jnp.bfloat16)

    for step, (top, vector, count) in enumerate(steps):
        fetch(step).wait()
        for strip in range(strips):
            start = top + strip * STRIP
            product = jnp.dot(
                left[:, vector * STRIP:(vector + count) * STRIP],
                slab[vector:vector + count, start:start + STRIP].reshape(count * STRIP, columns),
                preferred_element_type=jnp.float32,
            )
            if vector == 0:
                total[strip] = product
            else:
                total[strip] += product
        if vector + count == vectors:
            for w in range(walkers):
                out_ref[w, top:top + height] = jnp.concatenate(
                    [total[strip, w * STRIP:(w + 1) * STRIP] for strip in range(strips)], axis=0
                ).astype(jnp.bfloat16)


def potential_rows(shifted, slab, rows):
    walkers, blocks, _ = shifted.shape
    vectors, rows_here, columns = slab.shape
    height = min(16, rows)
    steps = slab_steps(vectors, rows, height)
    scratch = 2 * vectors * rows * columns + 2 * walkers * STRIP * (vectors * STRIP + 2 * (height // STRIP) * columns)
    return pl.pallas_call(
        functools.partial(potential_kernel, rows_here // rows, steps),
        in_specs=[pl.BlockSpec(memory_space=pltpu.VMEM), pl.BlockSpec(memory_space=pl.ANY)],
        out_shape=jax.ShapeDtypeStruct((walkers, rows, columns), jnp.bfloat16),
        scratch_shapes=[
            pltpu.VMEM((vectors, rows, columns), slab.dtype),
            pltpu.VMEM(shifted.shape, jnp.float32),
            pltpu.VMEM((walkers * STRIP, vectors * STRIP), jnp.bfloat16),
            pltpu.VMEM((height // STRIP, walkers * STRIP, columns), jnp.float32),
            pltpu.SemaphoreType.DMA((len(steps),)),
        ],
        compiler_params=pltpu.CompilerParams(vmem_limit_bytes=scratch + (8 if rows < rows_here else 24) * MIB),
        cost_estimate=pl.CostEstimate(
            flops=2 * walkers * STRIP * rows * vectors * columns,
            bytes_accessed=2 * rows * vectors * columns,
            transcendentals=0,
        ),
    )(shifted, slab)


def taylor_kernel(blocks_ref, onebody_ref, walker_ref, out_ref, matrix, diagonal, terms, result, sent):
    kpoints, shares, rows, size = blocks_ref.shape
    orbitals = size // kpoints
    columns = walker_ref.shape[1]
    per_tile = LANES // orbitals
    own = (
        lax.broadcasted_iota(jnp.int32, (orbitals, orbitals), 0)
        == lax.broadcasted_iota(jnp.int32, (orbitals, orbitals), 1)
    )

    turned = {}

    def piece(q, s, k, place):
        tile, at = divmod(k, per_tile)
        lanes = slice(tile * LANES, (tile + 1) * LANES)
        shift = (place - at) % per_tile * orbitals
        key = (q, s, tile, shift)
        if key not in turned:
            block = blocks_ref[q, s, :, lanes]
            turned[key] = jnp.concatenate([block[:, LANES - shift:], block[:, :LANES - shift]], axis=1) if shift else block
        return turned[key][:, place * orbitals:(place + 1) * orbitals]

    def arrange(k):
        lanes = slice(k * orbitals, (k + 1) * orbitals)
        for tile in range(kpoints // per_tile):
            sources = [(k - tile * per_tile - i) % kpoints for i in range(per_tile)]
            for s in range(shares):
                top = k * orbitals + s * rows
                matrix[top:top + rows, tile * LANES:(tile + 1) * LANES] = jnp.concatenate(
                    [piece(q, s, k, place) for place, q in enumerate(sources)], axis=1
                )
        column = jnp.sum(jnp.where(own, onebody_ref[k:k + 1], 0.0), axis=1, keepdims=True)
        diagonal[lanes] = jnp.broadcast_to(column, (orbitals, LANES))

    def send(first):
        band = pl.ds(first * orbitals, BAND * orbitals)
        return pltpu.make_async_copy(result.at[band], out_ref.at[band], sent.at[first // BAND])

    for order in range(1, TERMS):
        before = walker_ref if order == 1 else terms.at[order - 2]
        for first in range(0, kpoints, BAND):
            band = slice(first * orbitals, (first + BAND) * orbitals)
            if order == 1:
                for k in range(first, first + BAND):
                    arrange(k)
            product = jnp.dot(matrix[band], before[...], preferred_element_type=jnp.float32)
            here = before[band].astype(jnp.float32)
            product += jnp.concatenate([diagonal[band]] * (columns // LANES), axis=1) * here
            value = (product * (-1.0 / order)).astype(jnp.bfloat16)
            if order < TERMS - 1:
                terms[order - 1, band] = value
            else:
                total = walker_ref[band].astype(jnp.float32)
                for n in range(TERMS - 2):
                    total += terms[n, band].astype(jnp.float32)
                result[band] = (total + value.astype(jnp.float32)).astype(jnp.bfloat16)
                send(first).start()
    for first in range(0, kpoints, BAND):
        send(first).wait()


def taylor(blocks, onebody, walker):
    kpoints, _ = onebody.shape
    size, columns = walker.shape
    return pl.pallas_call(
        taylor_kernel,
        out_specs=pl.BlockSpec(memory_space=pl.ANY),
        out_shape=jax.ShapeDtypeStruct(walker.shape, jnp.bfloat16),
        scratch_shapes=[
            pltpu.VMEM((size, size), jnp.bfloat16),
            pltpu.VMEM((size, LANES), jnp.float32),
            pltpu.VMEM((TERMS - 2, size, columns), jnp.bfloat16),
            pltpu.VMEM((size, columns), jnp.bfloat16),
            pltpu.SemaphoreType.DMA((kpoints // BAND,)),
        ],
        compiler_params=pltpu.CompilerParams(vmem_limit_bytes=24 * MIB),
        cost_estimate=pl.CostEstimate(
            flops=2 * (TERMS - 1) * size * size * columns,
            bytes_accessed=2 * size * (size + 2 * columns),
            transcendentals=0,
        ),
    )(blocks, onebody, walker)


def exchange(blocks, axes):
    return lax.all_to_all(blocks, axes, split_axis=0, concat_axis=0, tiled=True)


def per_device(fields, field_shift, cholesky, onebody, walkers):
    devices, groups = lax.axis_size("pb"), lax.axis_size("groups")
    local_walkers = fields.shape[0]
    kpoints, orbitals = onebody.shape
    vectors, rows_here, columns = cholesky.shape
    per_transfer = orbitals // rows_here

    shares = groups if local_walkers == 1 and per_transfer == 1 and rows_here % (16 * groups) == 0 else 1
    axes = ("pb", "groups") if shares > 1 else "pb"
    rows = rows_here // shares
    outgoing = [shift_fields(fields[w], field_shift, shares) for w in range(local_walkers)]
    outgoing = jnp.repeat(jnp.stack(outgoing, axis=2), per_transfer, axis=0)
    arrived = exchange(outgoing.reshape((devices * shares,) + outgoing.shape[2:]), axes)
    arrived = arrived.reshape((devices * shares * local_walkers,) + arrived.shape[2:])

    blocks = potential_rows(arrived, cholesky, rows)
    relayed = exchange(blocks.reshape(devices * shares, local_walkers, rows, columns), axes)
    results = [
        taylor(relayed[:, w].reshape(kpoints, shares, per_transfer * rows, columns), onebody, walkers[w])
        for w in range(local_walkers)
    ]
    return jnp.stack(results, axis=0)


def solution(mesh):
    return jax.shard_map(
        per_device,
        mesh=mesh,
        in_specs=(
            P(("groups", "pb"), None, None),
            P(),
            P(None, "pb", None),
            P(),
            P(("groups", "pb"), None, None),
        ),
        out_specs=P(("groups", "pb"), None, None),
        check_vma=False,
    )
```
